512 devices in a mesh: traj: 32 (over z_hi, y, core), tm: 16 (over z_lo, x).
Axes of the slice: x: 4, y: 4, z: 16 (z_hi: 4, z_lo: 4; z = z_hi * 4 + z_lo), core: 2. Of those that a mesh axis runs over, the one named last changes fastest.
Arguments:
- states: float32 [16, 32, 8192], P('tm', None, 'traj'), may hold values from -6 to 6
- vectors: bfloat16 [64, 8192], P(None, 'traj'), may hold values from -6 to 6
- kernel_scale: float32 [16], P('tm'), may hold values from 6 to 16
- neighbour_blocks: int32 [64, 24], P('traj'), may hold values from 0 to 63, as said below
- neighbour_count: int32 [64], P('traj'), may hold values from 6 to 24, as said below
Outputs:
- result: float32 [64, 8192], P(None, 'traj')
The draws below stay inside these ranges and needn't reach their ends.
Inputs may be any that keep to these rules, and one draw needn't show every extreme that they name: `neighbour_blocks`: row b names 24 different blocks, the first of them b itself. Only the first neighbour_count[b] entries of row b of neighbour_blocks are neighbours of block b; some block uses all 24.
All inputs are finite; a program needn't handle non-finite values.
Results may differ from the reference program's by a relative error of at most 0.0013.
Values may be sent and summed in bfloat16 or wider, within the bound.
A program may use at most 64 MiB of HBM per device.

```python
import math
import jax
import jax.numpy as jnp
from jax import lax

COORD = 32
VECS = 64
BLK = 128
NBR = 24
SLICES = 16
TRAJ_ALL = 8192
BLOCKS = 64


def draw_neighbour_blocks(key, part):
    keys = jax.random.split(jax.random.fold_in(key, 11), BLOCKS)

    def one_row(row_key):
        return jax.random.permutation(row_key, BLOCKS - 1)[:NBR - 1].astype(jnp.int32) + 1
    offsets = jax.vmap(one_row)(keys)
    owners = jnp.arange(BLOCKS, dtype=jnp.int32)[:, None]
    others = (owners + offsets) % BLOCKS
    return jnp.concatenate([owners, others], axis=1).astype(jnp.int32)


def draw_neighbour_count(key, part):
    lowest = max(NBR // 4, 1)
    spread = NBR - lowest
    raw = jax.random.randint(jax.random.fold_in(key, 12), (BLOCKS,), 0, spread + 1)
    counts = lowest + raw * raw * raw // max(spread * spread, 1)
    chosen = jax.random.randint(jax.random.fold_in(key, 13), (), 0, BLOCKS)
    counts = counts.at[chosen].set(NBR)
    return counts.astype(jnp.int32)


def steps_of(own_key, extent, cuts, least, high):
    level, own = 1.0, jax.random.fold_in(own_key, 6)
    for position, parts in cuts:
        steps = jnp.exp(jax.random.uniform(jax.random.fold_in(own, position), (parts,), jnp.float32, least / len(cuts), high / len(cuts)))
        level = level * jnp.repeat(steps, extent[position] // parts).reshape([-1 if axis == position else 1 for axis in range(len(extent))])
    return level


def bell_draw(key, dims, deviation, most, pieces=(), kind=jnp.bfloat16):
    entries = deviation * jax.random.normal(key, dims, jnp.float32)
    if pieces:
        entries = entries * steps_of(key, dims, pieces, -0.22, 0.18)
    return jnp.clip(entries, -most, most).astype(kind)


def setup_inputs(seed: int = 0) -> dict:
    key_of = jax.random.split(jax.random.key(seed), 6)
    return {
        "states": bell_draw(key_of[0], (SLICES, COORD, TRAJ_ALL), 1.0, 6.0, ((0, 16), (2, 32)), jnp.float32),
        "vectors": bell_draw(key_of[1], (VECS, TRAJ_ALL), 1.0, 6.0, ((1, 32),)),
        "kernel_scale": jnp.clip(jnp.exp(math.log(16.0) - 0.98082925 * jax.random.uniform(key_of[2], (SLICES,), jnp.float32) ** steps_of(key_of[2], (SLICES,), ((0, 16),), -0.2, 0.2)), 6.0, 16.0),
        "neighbour_blocks": draw_neighbour_blocks(jax.random.fold_in(key_of[5], 71), 0),
        "neighbour_count": draw_neighbour_count(jax.random.fold_in(key_of[5], 71), 0),
    }


def linked_blocks(neighbour_blocks, neighbour_count, blocks_total):
    slots = neighbour_blocks.shape[1]
    named = neighbour_blocks[:, :, None] == jnp.arange(blocks_total, dtype=jnp.int32)[None, None, :]
    within = jnp.arange(slots, dtype=jnp.int32)[None, :, None] < neighbour_count[:, None, None]
    return jnp.any(named & within, axis=1).astype(jnp.float32)


def reference(states, vectors, kernel_scale, neighbour_blocks, neighbour_count):
    columns = states.shape[2]
    blocks_total = columns // BLK
    linked = linked_blocks(neighbour_blocks, neighbour_count, blocks_total)

    def one_slice(running, slice_index):
        coords = states[slice_index]
        squares = jnp.sum(coords * coords, axis=0)
        spread = kernel_scale[slice_index]

        def one_block(running_block, block_index):
            row_start = (block_index * BLK).astype(jnp.int32)
            rows = lax.dynamic_slice_in_dim(coords, row_start, BLK, 1)
            cross = jnp.dot(rows.T, coords, precision=lax.Precision.HIGHEST)
            row_squares = lax.dynamic_slice_in_dim(squares, row_start, BLK, 0)
            distance = row_squares[:, None] + squares[None, :] - 2.0 * cross
            mask = jnp.repeat(linked[block_index], BLK)
            kernel = mask[None, :] * jnp.exp(-distance / spread)
            row_sum = jnp.sum(kernel, axis=1)
            weights = kernel.astype(jnp.bfloat16)
            pushed = lax.dot_general(vectors, weights, (((1,), (1,)), ((), ())), preferred_element_type=jnp.float32)
            scaled = (pushed / (row_sum * row_sum)[None, :]).astype(jnp.bfloat16)
            pulled = jnp.dot(scaled, weights, preferred_element_type=jnp.float32)
            return running_block + pulled, None

        running, unused = lax.scan(one_block, running, jnp.arange(blocks_total, dtype=jnp.int32))
        return running, None

    initial = jnp.zeros((vectors.shape[0], columns), jnp.float32)
    result, unused = lax.scan(one_slice, initial, jnp.arange(states.shape[0], dtype=jnp.int32))
    return result
```

```python
import functools
import math

import jax
import jax.numpy as jnp
from jax import lax
from jax.experimental import pallas as pl
from jax.experimental.pallas import tpu as pltpu
from jax.sharding import PartitionSpec as P

MESH = pl.DeviceIdType.MESH
BLK = 128
STEP = 5461.0
NONE = -1


def wait_for(ref, sem):
    pltpu.make_async_copy(ref, ref, sem).wait()


def digits(codes):
    high = (codes + 128) >> 8
    low = codes - (high << 8)
    return (high << 8).astype(jnp.float32), low.astype(jnp.float32)


def three_parts(value):
    one = value.astype(jnp.bfloat16).astype(jnp.float32)
    two = (value - one).astype(jnp.bfloat16).astype(jnp.float32)
    return one, two, value - one - two


def augmented(codes, times, order, first):
    whole = codes.astype(jnp.int32)
    high, low = digits(whole)
    real = whole.astype(jnp.float32)
    square = jnp.sum(real * real, axis=0, keepdims=True)
    row = lax.broadcasted_iota(jnp.int32, (16, codes.shape[1]), 0)
    extra = jnp.where((row >= 3 - first) & (row < 6 - first), 1.0, 0.0)
    for k, part in enumerate(three_parts(square)):
        extra = jnp.where(row == first + k, part, extra)
    both = {"h": (high * times).astype(jnp.bfloat16), "l": (low * times).astype(jnp.bfloat16)}
    return jnp.concatenate([both[k] for k in order] + [extra.astype(jnp.bfloat16)], axis=0)


def kernel(
    side,
    slices,
    states,
    vectors,
    scale,
    lists,
    counts,
    out,
    st_all,
    st_pair,
    ls_all,
    ls_pair,
    ve_all,
    sc_all,
    basis,
    mask_1,
    mask_2,
    first,
    second,
    row_sum,
    total,
    px_out,
    px_in,
    rs_out,
    rs_in,
    ag,
    st_send,
    st_recv,
    ls_send,
    ls_recv,
    ve_send,
    ve_recv,
    sc_send,
    sc_recv,
    pair_send,
    pair_recv,
    rs_send,
    rs_recv,
    ag_send,
    ag_recv,
    local_sem,
):
    chips = side * side
    traj, tm = lax.axis_index("traj"), lax.axis_index("tm")
    core, chip = traj % 2, traj // 2
    y, zh = chip % side, chip // side
    own = states.shape[1]
    vecs = vectors.shape[0]
    blocks = own // BLK

    def place(dz, dy):
        return ((zh + dz) % side) * side + (y + dy) % side

    def at(where, other=0):
        return {"traj": where * 2 + (core + other) % 2, "tm": tm}

    def at_slice(d):
        return {"traj": traj, "tm": (tm + d) % slices}

    near = [(0, d) for d in range(1, side)]
    far = [(d, 0) for d in range(1, side)]

    barrier = pltpu.get_barrier_semaphore()
    for dz, dy in far + near:
        pl.semaphore_signal(barrier, inc=1, device_id=at(place(dz, dy)), device_id_type=MESH)
    pl.semaphore_signal(barrier, inc=1, device_id=at(chip, 1), device_id_type=MESH)
    for d in range(1, slices):
        pl.semaphore_signal(barrier, inc=1, device_id=at_slice(d), device_id_type=MESH)

    local = pltpu.make_async_copy(vectors, ve_all.at[chip], local_sem)
    local.start()
    st_all[chip] = jnp.round(states[...] * STEP).astype(jnp.int32).astype(jnp.int16)
    ls_all[chip] = jnp.full((8, 128), NONE, jnp.int32)
    slot = lax.broadcasted_iota(jnp.int32, (1, lists.shape[1]), 1)
    for b in range(blocks):
        ls_all[chip, b : b + 1, : lists.shape[1]] = jnp.where(
            slot < counts[b], lists[b : b + 1, :], NONE
        )
    pl.semaphore_wait(barrier, 2 * side - 1 + slices - 1)

    def copy(src, dst, send, recv, device):
        return pltpu.make_async_remote_copy(
            src_ref=src, dst_ref=dst, send_sem=send, recv_sem=recv, device_id=device, device_id_type=MESH
        )

    def send_own(everyone, send, recv):
        for k, (dz, dy) in enumerate(far + near):
            copy(
                everyone.at[chip], everyone.at[chip], send.at[k], recv.at[chip], at(place(dz, dy))
            ).start()

    def forward(everyone, send, recv, dz):
        where = place(dz, 0)
        wait_for(everyone.at[where], recv.at[where])
        for k in range(1, side):
            copy(
                everyone.at[where],
                everyone.at[where],
                send.at[(dz + 1) * (side - 1) + k - 1],
                recv.at[where],
                at(place(0, k)),
            ).start()

    def all_sent(everyone, send):
        for k in range(chips - 1):
            wait_for(everyone.at[0], send.at[k])

    def pair(src, dst, k):
        return copy(src, dst, pair_send.at[k], pair_recv.at[k], at(chip, 1))

    send_own(st_all, st_send, st_recv)
    st_swap = pair(st_all.at[chip], st_pair, 0)
    st_swap.start()
    send_own(ls_all, ls_send, ls_recv)
    ls_swap = pair(ls_all.at[chip], ls_pair, 1)
    ls_swap.start()
    local.wait()
    send_own(ve_all, ve_send, ve_recv)

    hops = [1, side - 1] + list(range(2, side - 1)) if side > 2 else [1]
    for dz in hops:
        forward(st_all, st_send, st_recv, dz)
        forward(ls_all, ls_send, ls_recv, dz)

    basis[:, :own] = augmented(st_all[chip], -2.0, "hlhl", 3)
    st_swap.wait_recv()
    basis[:, own:] = augmented(st_pair[...], -2.0, "hlhl", 3)
    ls_swap.wait_recv()
    row_sum[...] = jnp.zeros_like(row_sum)
    rate = -math.log2(math.e) / (STEP * STEP) / scale[0]

    def build(where):
        base = 4 * where + 2 * core
        entry = lax.broadcasted_iota(jnp.int32, (8, 128), 0)
        there = ls_all[where]
        for b in range(2 * blocks):
            held = ls_all[chip] if b < blocks else ls_pair[...]
            mine = held[b % blocks : b % blocks + 1, :]
            name = 4 * chip + 2 * ((core + b // blocks) % 2) + b % blocks
            lanes = slice(b * BLK, (b + 1) * BLK)
            hit_1 = jnp.where(mine == base + entry, 1.0, 0.0)
            hit_2 = jnp.where(there == name, 1.0, 0.0)
            mask_1[where, :, lanes] = jnp.broadcast_to(
                jnp.max(hit_1, axis=1, keepdims=True), (8, BLK)
            )
            mask_2[where, :, lanes] = jnp.broadcast_to(
                jnp.max(hit_2, axis=1, keepdims=True), (8, BLK)
            )
        rows = augmented(st_all[where], 1.0, "hhll", 0)
        for h in range(blocks):
            part = slice(h * BLK, (h + 1) * BLK)
            distance = lax.dot_general(
                rows[:, part],
                basis[...],
                (((0,), (0,)), ((), ())),
                preferred_element_type=jnp.float32,
            )
            weight = jnp.exp2(distance * rate)
            linked = weight * mask_1[where, h : h + 1, :]
            row_sum[...] += jnp.sum(linked.reshape(BLK // 8, 8, 2 * own), axis=0)
            first[where, part, :] = linked.astype(jnp.bfloat16)
            second[where, part, :] = (weight * mask_2[where, h : h + 1, :]).astype(jnp.bfloat16)

    build(chip)
    for dz in [0] + hops:

        def one_build(dy, carry, dz=dz):
            where = place(dz, dy)
            wait_for(st_all.at[where], st_recv.at[where])
            wait_for(ls_all.at[where], ls_recv.at[where])
            build(where)
            return carry

        if dz:
            build(place(dz, 0))
        lax.fori_loop(1, side, one_build, 0)

    for dz in hops:
        forward(ve_all, ve_send, ve_recv, dz)

    def product(everyone, recv, weights):
        total[...] = jnp.zeros_like(total)
        for dz in [0] + hops:
            for dy in range(side):
                where = place(dz, dy)
                if dy:
                    wait_for(everyone.at[where], recv.at[where])
                total[...] += jnp.dot(
                    everyone[where], weights[where], preferred_element_type=jnp.float32
                )

    product(ve_all, ve_recv, first)
    px_out[0, :vecs] = total[:, own:]
    px_out[0, vecs:] = row_sum[:, own:]
    swap_1 = pair(px_out.at[0], px_in.at[0], 2)
    swap_1.start()
    swap_1.wait_recv()
    sums = jnp.sum(row_sum[:, :own] + px_in[0, vecs:], axis=0, keepdims=True)
    sc_all[chip] = ((total[:, :own] + px_in[0, :vecs]) / (sums * sums)).astype(jnp.bfloat16)

    send_own(sc_all, sc_send, sc_recv)
    for dz in hops:
        forward(sc_all, sc_send, sc_recv, dz)
    product(sc_all, sc_recv, second)
    px_out[1, :vecs] = total[:, own:]
    swap_2 = pair(px_out.at[1, pl.ds(0, vecs)], px_in.at[1, pl.ds(0, vecs)], 3)
    swap_2.start()
    swap_2.wait_recv()

    tiles = rs_out.shape[0]
    wide = own // 128
    per = tiles // slices
    for t in range(tiles):
        rows, lanes = slice(t // wide * 8, t // wide * 8 + 8), slice(t % wide * 128, t % wide * 128 + 128)
        rs_out[t] = total[rows, lanes] + px_in[1, rows, lanes]

    def scatter(d, carry):
        there = (tm + d) % slices
        copy(
            rs_out.at[pl.ds(there * per, per)], rs_in.at[tm], rs_send.at[d], rs_recv.at[tm], at_slice(d)
        ).start()
        return carry

    def scattered(d, carry):
        there = (tm + d) % slices
        wait_for(rs_in.at[there], rs_recv.at[there])
        return carry

    lax.fori_loop(1, slices, scatter, 0)
    rs_in[tm] = rs_out[pl.ds(tm * per, per)]
    lax.fori_loop(1, slices, scattered, 0)
    ag[tm] = jnp.sum(rs_in[...], axis=0)

    def spread(d, carry):
        copy(ag.at[tm], ag.at[tm], ag_send.at[d], ag_recv.at[tm], at_slice(d)).start()
        return carry

    def arrived(d, carry):
        there = (tm + d) % slices
        wait_for(ag.at[there], ag_recv.at[there])
        return carry

    lax.fori_loop(1, slices, spread, 0)
    lax.fori_loop(1, slices, arrived, 0)
    for t in range(tiles):
        rows, lanes = slice(t // wide * 8, t // wide * 8 + 8), slice(t % wide * 128, t % wide * 128 + 128)
        out[rows, lanes] = ag[t // per, t % per]

    all_sent(st_all, st_send)
    all_sent(ls_all, ls_send)
    all_sent(ve_all, ve_send)
    all_sent(sc_all, sc_send)
    for swap in (st_swap, ls_swap, swap_1, swap_2):
        swap.wait_send()

    def sent(d, carry):
        wait_for(rs_in.at[0], rs_send.at[d])
        wait_for(ag.at[0], ag_send.at[d])
        return carry

    lax.fori_loop(1, slices, sent, 0)


def per_device(side, slices, states, vectors, kernel_scale, neighbour_blocks, neighbour_count):
    coords, own = states.shape[1:]
    vecs = vectors.shape[0]
    chips = side * side
    tiles = vecs * own // 1024
    vmem = pl.BlockSpec(memory_space=pltpu.VMEM)
    smem = pl.BlockSpec(memory_space=pltpu.SMEM)
    dma = pltpu.SemaphoreType.DMA
    return pl.pallas_call(
        functools.partial(kernel, side, slices),
        out_shape=jax.ShapeDtypeStruct((vecs, own), jnp.float32),
        in_specs=[vmem, vmem, smem, vmem, smem],
        out_specs=vmem,
        scratch_shapes=[
            pltpu.VMEM((chips, coords, own), jnp.int16),
            pltpu.VMEM((coords, own), jnp.int16),
            pltpu.VMEM((chips, 8, 128), jnp.int32),
            pltpu.VMEM((8, 128), jnp.int32),
            pltpu.VMEM((chips, vecs, own), jnp.bfloat16),
            pltpu.VMEM((chips, vecs, own), jnp.bfloat16),
            pltpu.VMEM((4 * coords + 16, 2 * own), jnp.bfloat16),
            pltpu.VMEM((chips, 8, 2 * own), jnp.float32),
            pltpu.VMEM((chips, 8, 2 * own), jnp.float32),
            pltpu.VMEM((chips, own, 2 * own), jnp.bfloat16),
            pltpu.VMEM((chips, own, 2 * own), jnp.bfloat16),
            pltpu.VMEM((8, 2 * own), jnp.float32),
            pltpu.VMEM((vecs, 2 * own), jnp.float32),
            pltpu.VMEM((2, vecs + 8, own), jnp.float32),
            pltpu.VMEM((2, vecs + 8, own), jnp.float32),
            pltpu.VMEM((tiles, 8, 128), jnp.float32),
            pltpu.VMEM((slices, tiles // slices, 8, 128), jnp.float32),
            pltpu.VMEM((slices, tiles // slices, 8, 128), jnp.float32),
            dma((chips,)),
            dma((chips,)),
            dma((chips,)),
            dma((chips,)),
            dma((chips,)),
            dma((chips,)),
            dma((chips,)),
            dma((chips,)),
            dma((4,)),
            dma((4,)),
            dma((slices,)),
            dma((slices,)),
            dma((slices,)),
            dma((slices,)),
            dma,
        ],
        compiler_params=pltpu.CompilerParams(
            collective_id=0, has_side_effects=True, vmem_limit_bytes=40 * 1024 * 1024
        ),
    )(states.reshape(coords, own), vectors, kernel_scale, neighbour_blocks, neighbour_count)


def solution(mesh):
    side, slices = math.isqrt(mesh.shape["traj"] // 2), mesh.shape["tm"]
    return jax.shard_map(
        functools.partial(per_device, side, slices),
        mesh=mesh,
        in_specs=(P("tm", None, "traj"), P(None, "traj"), P("tm"), P("traj", None), P("traj")),
        out_specs=P(None, "traj"),
        check_vma=False,
    )
```

```python
import functools
import math

import jax
import jax.numpy as jnp
from jax import lax
from jax.experimental import pallas as pl
from jax.experimental.pallas import tpu as pltpu
from jax.sharding import PartitionSpec as P

MESH = pl.DeviceIdType.MESH
BLK = 128
FO = 0
SO = 3
VL = 32
STEP = 5461.0
NONE = -1


def wait_for(ref, sem):
    pltpu.make_async_copy(ref, ref, sem).wait()


def digits(codes):
    high = (codes + 128) >> 8
    low = codes - (high << 8)
    return (high << 8).astype(jnp.float32), low.astype(jnp.float32)


def three_parts(value):
    one = value.astype(jnp.bfloat16).astype(jnp.float32)
    two = (value - one).astype(jnp.bfloat16).astype(jnp.float32)
    return one, two, value - one - two


def augmented(codes, times, order, first):
    whole = codes.astype(jnp.int32)
    high, low = digits(whole)
    real = whole.astype(jnp.float32)
    square = jnp.sum(real * real, axis=0, keepdims=True)
    row = lax.broadcasted_iota(jnp.int32, (16, codes.shape[1]), 0)
    extra = jnp.where((row >= 3 - first) & (row < 6 - first), 1.0, 0.0)
    for k, part in enumerate(three_parts(square)):
        extra = jnp.where(row == first + k, part, extra)
    both = {"h": (high * times).astype(jnp.bfloat16), "l": (low * times).astype(jnp.bfloat16)}
    return jnp.concatenate([both[k] for k in order] + [extra.astype(jnp.bfloat16)], axis=0)


def kernel(
    side,
    xs,
    slices,
    states,
    vectors,
    scale_in,
    lists_in,
    counts_in,
    out,
    coords,
    scale,
    lists,
    counts,
    st_all,
    st_pair,
    ls_all,
    ls_pair,
    ve_all,
    sc_all,
    basis,
    mask_1,
    mask_2,
    first,
    second,
    row_sum,
    total,
    px_out,
    px_in,
    rs_out,
    rs_in,
    ag,
    st_send,
    st_recv,
    ls_send,
    ls_recv,
    vz_send,
    vz_recv,
    ve_send,
    ve_recv,
    sc_send,
    sc_recv,
    pair_send,
    pair_recv,
    rs_send,
    rs_recv,
    ag_send,
    ag_recv,
    local_sem,
):
    chips = side * side
    traj, tm = lax.axis_index("traj"), lax.axis_index("tm")
    core, chip = traj % 2, traj // 2
    y, zh = chip % side, chip // side
    own = states.shape[2]
    vecs = vectors.shape[0]
    half = ls_pair.shape[1] // 2
    blocks = own // BLK

    def place(dz, dy):
        return ((zh + dz) % side) * side + (y + dy) % side

    def at(where, other=0):
        return {"traj": where * 2 + (core + other) % 2, "tm": tm}

    def at_slice(d):
        return {"traj": traj, "tm": (tm + d) % slices}

    x, zl = tm % xs, tm // xs

    def in_plane(dx, dy):
        return {"traj": place(0, dy) * 2 + core, "tm": zl * xs + (x + dx) % xs}

    plane = [(dx, dy) for dx in range(xs) for dy in range(side) if dx or dy]
    plane.sort(key=lambda d: -min(d[0], xs - d[0]) - min(d[1], side - d[1]))
    thick = vecs // xs
    share = pl.ds(pl.multiple_of(x * thick, thick), thick)

    hops = sorted(range(1, side), key=lambda d: -min(d, side - d))
    near_first = hops[::-1]
    barrier = pltpu.get_barrier_semaphore()
    for d in hops:
        pl.semaphore_signal(barrier, inc=1, device_id=at(place(d, 0)), device_id_type=MESH)
    for dx, dy in plane:
        if dy:
            pl.semaphore_signal(barrier, inc=1, device_id=in_plane(dx, dy), device_id_type=MESH)
    pl.semaphore_signal(barrier, inc=1, device_id=at(chip, 1), device_id_type=MESH)
    for d in range(1, slices):
        pl.semaphore_signal(barrier, inc=1, device_id=at_slice(d), device_id_type=MESH)

    reads = [
        pltpu.make_async_copy(src, dst, local_sem.at[k])
        for k, (src, dst) in enumerate(
            (
                (states.at[0], coords),
                (lists_in, lists),
                (counts_in, counts),
                (scale_in, scale),
                (vectors, ve_all.at[chip]),
            )
        )
    ]
    for read in reads:
        read.start()
    row_sum[...] = jnp.zeros_like(row_sum)
    total[...] = jnp.zeros_like(total)
    for read in reads:
        read.wait()
    slot = lax.broadcasted_iota(jnp.int32, (1, lists.shape[1]), 1)
    ls_all[chip] = jnp.full((1, 2 * half), NONE, jnp.int32)
    for b in range(blocks):
        ls_all[chip, :, b * half : b * half + lists.shape[1]] = jnp.where(
            slot < counts[b], lists[b : b + 1, :], NONE
        )
    st_all[chip] = jnp.round(coords[...] * STEP).astype(jnp.int32).astype(jnp.int16)
    basis[:, :own] = augmented(st_all[chip], -2.0, "hlhl", 3)
    rate = -math.log2(math.e) / (STEP * STEP) / scale[0]
    pl.semaphore_wait(barrier, (side - 1) + (xs * side - xs) + 1 + slices - 1)

    def copy(src, dst, send, recv, device):
        return pltpu.make_async_remote_copy(
            src_ref=src, dst_ref=dst, send_sem=send, recv_sem=recv, device_id=device, device_id_type=MESH
        )

    def send_z(everyone, send, recv, d):
        mine = everyone.at[chip]
        copy(mine, mine, send, recv.at[chip], at(place(d, 0))).start()

    def send_y(everyone, send, recv):
        mine = everyone.at[chip]
        for d in hops:
            copy(mine, mine, send, recv.at[chip], at(place(0, d))).start()

    def forward(everyone, send, recv, dz):
        theirs = everyone.at[place(dz, 0)]
        arrived = recv.at[place(dz, 0)]
        wait_for(theirs, arrived)
        for d in hops:
            copy(theirs, theirs, send, arrived, at(place(0, d))).start()

    def all_sent(everyone, send):
        every = everyone.at[pl.ds(0, chips - 1)]
        wait_for(every, send)

    def send_share(d):
        mine = ve_all.at[chip, share]
        copy(mine, mine, vz_send, vz_recv.at[zh], at(place(d, 0))).start()

    def forward_share(d):
        there = place(d, 0)
        theirs = ve_all.at[there, share]
        wait_for(theirs, vz_recv.at[(zh + d) % side])
        for dx, dy in plane:
            copy(theirs, theirs, ve_send.at[d], ve_recv.at[there], in_plane(dx, dy)).start()

    def shares_sent():
        wait_for(ve_all.at[pl.ds(0, side - 1), pl.ds(0, thick)], vz_send)
        wait_for(ve_all.at[pl.ds(0, side - 1)], ve_send.at[0])
        for d in hops:
            wait_for(ve_all.at[pl.ds(0, len(plane)), pl.ds(0, thick)], ve_send.at[d])

    def share_wait(dz, dy):
        where = place(dz, dy)
        if dy:
            wait_for(ve_all.at[where], ve_recv.at[where])
        elif dz and xs > 1:
            wait_for(ve_all.at[where, pl.ds(0, vecs - thick)], ve_recv.at[where])

    def shard_wait(dz, dy):
        where = place(dz, dy)
        if dy:
            wait_for(sc_all.at[where], sc_recv.at[where])

    def pair(src, dst, k):
        return copy(src, dst, pair_send.at[k], pair_recv.at[k], at(chip, 1))

    st = (st_all, st_send, st_recv)
    ls = (ls_all, ls_send, ls_recv)
    sc = (sc_all, sc_send, sc_recv)
    near, far = near_first[:-1], near_first[-1]
    if FO == 0:
        first_steps = [(w, d) for w in ("st", "ls", "ve") for d in hops + [0]]
    elif FO == 1:
        first_steps = [("st", d) for d in hops] + [("ls", d) for d in hops] + [("st", 0), ("ls", 0)] + [("ve", d) for d in hops + [0]]
    elif FO == 2:
        first_steps = [("st", far), ("ls", far), ("ve", far)] + [(w, d) for w in ("st", "ls") for d in near + [0]] + [("ve", d) for d in near + [0]]
    elif FO == 3:
        first_steps = [("st", far), ("ls", far)] + [(w, d) for w in ("st", "ls") for d in near + [0]] + [("ve", d) for d in [0] + near + [far]]
    for what, d in first_steps:
        group = {"st": st, "ls": ls, "ve": (ve_all, ve_send.at[0], ve_recv)}[what]
        if d:
            send_share(d) if what == "ve" else send_z(*group, d)
        else:
            send_y(*group)
        if what == "st" and not d:
            st_swap = pair(st_all.at[chip], st_pair, 0)
            ls_swap = pair(ls_all.at[chip], ls_pair, 1)
            st_swap.start()
            ls_swap.start()
    def build(where):
        base = 4 * where + 2 * core
        entry = lax.broadcasted_iota(jnp.int32, (8, 2 * half), 0)
        lane = lax.broadcasted_iota(jnp.int32, (8, 2 * half), 1)
        block = lane // half
        there = jnp.where(entry == block, jnp.broadcast_to(ls_all[where], (8, 2 * half)), NONE)
        for b in range(2 * blocks):
            held = ls_all[chip] if b < blocks else ls_pair[...]
            mine = jnp.where(block == b % blocks, jnp.broadcast_to(held, (8, 2 * half)), NONE)
            name = 4 * chip + 2 * ((core + b // blocks) % 2) + b % blocks
            lanes = slice(b * BLK, (b + 1) * BLK)
            for mask, hit in ((mask_1, mine == base + entry), (mask_2, there == name)):
                found = jnp.max(jnp.where(hit, 1.0, 0.0), axis=1, keepdims=True)
                mask[where, :, lanes] = jnp.broadcast_to(found, (8, BLK))
        rows = augmented(st_all[where], 1.0, "hhll", 0)
        for h in range(blocks):
            part = slice(h * BLK, (h + 1) * BLK)
            distance = lax.dot_general(
                rows[:, part],
                basis[...],
                (((0,), (0,)), ((), ())),
                preferred_element_type=jnp.float32,
            )
            weight = jnp.exp2(distance * rate)
            linked = weight * mask_1[where, h : h + 1, :]
            row_sum[...] += jnp.sum(linked.reshape(BLK // 8, 8, 2 * own), axis=0)
            first[where, part, :] = linked.astype(jnp.bfloat16)
            second[where, part, :] = (weight * mask_2[where, h : h + 1, :]).astype(jnp.bfloat16)

    def builds(dz):
        build(place(dz, 0))

        def body(dy, carry):
            where = place(dz, dy)
            wait_for(st_all.at[where], st_recv.at[where])
            wait_for(ls_all.at[where], ls_recv.at[where])
            build(where)
            return carry

        lax.fori_loop(1, side, body, 0)

    def products(everyone, arrive, weights, dz, cores=(1, 0), wait=True):
        for c in cores:
            part = slice(c * own, (c + 1) * own)
            sums = total[:, part]
            for dy in range(side):
                where = place(dz, dy)
                if wait and c == cores[0]:
                    arrive(dz, dy)
                sums = sums + jnp.dot(
                    everyone[where], weights[where, :, part], preferred_element_type=jnp.float32
                )
            total[:, part] = sums

    if SO == 0:
        second_steps = [("fs", d) for d in near] + [("b0", 0), ("b", 0), ("fs", far)] + [("b", d) for d in near] + [("fv", d) for d in near] + [("p", 0), ("b", far), ("fv", far)] + [("p", d) for d in near]
    elif SO == 1:
        second_steps = [("fs", d) for d in near] + [("b0", 0), ("b", 0)] + [("b", d) for d in near] + [("fs", far)] + [("fv", d) for d in near] + [("p", 0), ("b", far), ("fv", far)] + [("p", d) for d in near]
    elif SO == 2:
        second_steps = [("fs", d) for d in near] + [("b0", 0), ("b", 0), ("fs", far), ("fv", near[0])] + [("b", d) for d in near] + [("fv", near[-1])] + [("p", 0), ("fv", far), ("b", far)] + [("p", d) for d in near]
    elif SO == 3:
        second_steps = [("fs", d) for d in near] + [("b0", 0), ("b", 0), ("fs", far)] + [("fv", d) for d in near] + [("b", d) for d in near] + [("fv", far), ("p", 0), ("b", far)] + [("p", d) for d in near]
    for step, dz in second_steps:
        if step == "fs":
            forward(*st, dz)
            forward(*ls, dz)
        elif step == "b0":
            st_swap.wait_recv()
            basis[:, own:] = augmented(st_pair[...], -2.0, "hlhl", 3)
            ls_swap.wait_recv()
        elif step == "b":
            builds(dz)
        elif step == "fv":
            forward_share(dz)
        elif step == "p":
            products(ve_all, share_wait, first, dz)

    products(ve_all, share_wait, first, far, (1,))
    px_out[0, :vecs] = total[:, own:]
    px_out[0, vecs:] = row_sum[:, own:]
    swap_1 = pair(px_out.at[0], px_in.at[0], 2)
    swap_1.start()
    products(ve_all, share_wait, first, far, (0,), False)
    swap_1.wait_recv()
    sums = jnp.sum(row_sum[:, :own] + px_in[0, vecs:], axis=0, keepdims=True)
    sc_all[chip] = ((total[:, :own] + px_in[0, :vecs]) / (sums * sums)).astype(jnp.bfloat16)
    for d in hops:
        send_z(*sc, d)
    send_y(*sc)
    total[...] = jnp.zeros_like(total)
    for dz in near:
        forward(*sc, dz)
    products(sc_all, shard_wait, second, 0)
    forward(*sc, far)
    for dz in near:
        products(sc_all, shard_wait, second, dz)
    products(sc_all, shard_wait, second, far, (1,))
    px_out[1, :vecs] = total[:, own:]
    swap_2 = pair(px_out.at[1, pl.ds(0, vecs)], px_in.at[1, pl.ds(0, vecs)], 3)
    swap_2.start()
    products(sc_all, shard_wait, second, far, (0,), False)
    swap_2.wait_recv()

    tiles = rs_out.shape[0]
    wide = own // 128
    per = tiles // slices
    for t in range(tiles):
        rows, lanes = slice(t // wide * 8, t // wide * 8 + 8), slice(t % wide * 128, t % wide * 128 + 128)
        rs_out[t] = total[rows, lanes] + px_in[1, rows, lanes]

    for d in range(1, slices):
        there = (tm + d) % slices
        copy(
            rs_out.at[pl.ds(there * per, per)], rs_in.at[tm], rs_send, rs_recv.at[tm], at_slice(d)
        ).start()

    def scattered(d, carry):
        there = (tm + d) % slices
        wait_for(rs_in.at[there], rs_recv.at[there])
        return carry

    rs_in[tm] = rs_out[pl.ds(tm * per, per)]
    lax.fori_loop(1, slices, scattered, 0)
    ag[tm] = jnp.sum(rs_in[...], axis=0)

    for d in range(1, slices):
        copy(ag.at[tm], ag.at[tm], ag_send, ag_recv.at[tm], at_slice(d)).start()

    def arrived(d, carry):
        there = (tm + d) % slices
        wait_for(ag.at[there], ag_recv.at[there])
        return carry

    lax.fori_loop(1, slices, arrived, 0)
    for t in range(tiles):
        rows, lanes = slice(t // wide * 8, t // wide * 8 + 8), slice(t % wide * 128, t % wide * 128 + 128)
        out[rows, lanes] = ag[t // per, t % per]

    all_sent(st_all, st_send)
    all_sent(ls_all, ls_send)
    shares_sent()
    all_sent(sc_all, sc_send)
    for swap in (st_swap, ls_swap, swap_1, swap_2):
        swap.wait_send()

    wait_for(rs_in.at[pl.ds(0, slices - 1)], rs_send)
    wait_for(ag.at[pl.ds(0, slices - 1)], ag_send)


def per_device(side, xs, slices, states, vectors, kernel_scale, neighbour_blocks, neighbour_count):
    coords, own = states.shape[1:]
    vecs = vectors.shape[0]
    chips = side * side
    tiles = vecs * own // 1024
    vmem = pl.BlockSpec(memory_space=pltpu.VMEM)
    hbm = pl.BlockSpec(memory_space=pltpu.HBM)
    dma = pltpu.SemaphoreType.DMA
    return pl.pallas_call(
        functools.partial(kernel, side, xs, slices),
        out_shape=jax.ShapeDtypeStruct((vecs, own), jnp.float32),
        in_specs=[hbm] * 5,
        out_specs=vmem,
        scratch_shapes=[
            pltpu.VMEM((coords, own), jnp.float32),
            pltpu.SMEM((1,), jnp.float32),
            pltpu.VMEM(neighbour_blocks.shape, jnp.int32),
            pltpu.SMEM(neighbour_count.shape, jnp.int32),
            pltpu.VMEM((chips, coords, own), jnp.int16),
            pltpu.VMEM((coords, own), jnp.int16),
            pltpu.VMEM((chips, 1, 128), jnp.int32),
            pltpu.VMEM((1, 128), jnp.int32),
            pltpu.VMEM((chips, vecs, own), jnp.bfloat16),
            pltpu.VMEM((chips, vecs, own), jnp.bfloat16),
            pltpu.VMEM((4 * coords + 16, 2 * own), jnp.bfloat16),
            pltpu.VMEM((chips, 8, 2 * own), jnp.float32),
            pltpu.VMEM((chips, 8, 2 * own), jnp.float32),
            pltpu.VMEM((chips, own, 2 * own), jnp.bfloat16),
            pltpu.VMEM((chips, own, 2 * own), jnp.bfloat16),
            pltpu.VMEM((8, 2 * own), jnp.float32),
            pltpu.VMEM((vecs, 2 * own), jnp.float32),
            pltpu.VMEM((2, vecs + 8, own), jnp.float32),
            pltpu.VMEM((2, vecs + 8, own), jnp.float32),
            pltpu.VMEM((tiles, 8, 128), jnp.float32),
            pltpu.VMEM((slices, tiles // slices, 8, 128), jnp.float32),
            pltpu.VMEM((slices, tiles // slices, 8, 128), jnp.float32),
            dma,
            dma((chips,)),
            dma,
            dma((chips,)),
            dma,
            dma((side,)),
            dma((side,)),
            dma((chips,)),
            dma,
            dma((chips,)),
            dma((4,)),
            dma((4,)),
            dma,
            dma((slices,)),
            dma,
            dma((slices,)),
            dma((5,)),
        ],
        compiler_params=pltpu.CompilerParams(
            collective_id=0, has_side_effects=True, vmem_limit_bytes=VL * 1024 * 1024
        ),
    )(states, vectors, kernel_scale, neighbour_blocks, neighbour_count)


def solution(mesh):
    side, slices = math.isqrt(mesh.shape["traj"] // 2), mesh.shape["tm"]
    xs = min(side, slices)
    return jax.shard_map(
        functools.partial(per_device, side, xs, slices),
        mesh=mesh,
        in_specs=(P("tm", None, "traj"), P(None, "traj"), P("tm"), P("traj", None), P("traj")),
        out_specs=P(None, "traj"),
        check_vma=False,
    )
```

```python
import functools
import math

import jax
import jax.numpy as jnp
from jax import lax
from jax.experimental import pallas as pl
from jax.experimental.pallas import tpu as pltpu
from jax.sharding import PartitionSpec as P

MESH = pl.DeviceIdType.MESH
BLK = 128
VMEM_KIB = 55170
STEP = 5461.0
NONE = -1


def wait_for(ref, sem):
    pltpu.make_async_copy(ref, ref, sem).wait()


def digits(codes):
    high = (codes + 128) >> 8
    low = codes - (high << 8)
    return (high << 8).astype(jnp.float32), low.astype(jnp.float32)


def three_parts(value):
    one = value.astype(jnp.bfloat16).astype(jnp.float32)
    two = (value - one).astype(jnp.bfloat16).astype(jnp.float32)
    return one, two, value - one - two


def augmented(codes, times, order, first):
    whole = codes.astype(jnp.int32)
    high, low = digits(whole)
    real = whole.astype(jnp.float32)
    square = jnp.sum(real * real, axis=0, keepdims=True)
    row = lax.broadcasted_iota(jnp.int32, (16, codes.shape[1]), 0)
    extra = jnp.where((row >= 3 - first) & (row < 6 - first), 1.0, 0.0)
    for k, part in enumerate(three_parts(square)):
        extra = jnp.where(row == first + k, part, extra)
    both = {"h": (high * times).astype(jnp.bfloat16), "l": (low * times).astype(jnp.bfloat16)}
    return jnp.concatenate([both[k] for k in order] + [extra.astype(jnp.bfloat16)], axis=0)


def kernel(
    side,
    xs,
    slices,
    states,
    vectors,
    scale_in,
    lists_in,
    counts_in,
    out,
    coords,
    scale,
    lists,
    counts,
    st_all,
    st_pair,
    ls_all,
    ls_pair,
    ve_all,
    sc_all,
    basis,
    mask_1,
    mask_2,
    first,
    second,
    row_sum,
    total,
    px_out,
    px_in,
    rs_out,
    rs_in,
    ag,
    st_send,
    st_recv,
    ls_send,
    ls_recv,
    vz_send,
    vz_recv,
    ve_send,
    ve_recv,
    sc_send,
    sc_recv,
    pair_send,
    pair_recv,
    rs_send,
    rs_recv,
    ag_send,
    ag_recv,
    local_sem,
):
    chips = side * side
    traj, tm = lax.axis_index("traj"), lax.axis_index("tm")
    core, chip = traj % 2, traj // 2
    y, zh = chip % side, chip // side
    own = states.shape[2]
    vecs = vectors.shape[0]
    half = ls_pair.shape[1] // 2
    blocks = own // BLK

    def place(dz, dy):
        return ((zh + dz) % side) * side + (y + dy) % side

    def at(where, other=0):
        return {"traj": where * 2 + (core + other) % 2, "tm": tm}

    def at_slice(d):
        return {"traj": traj, "tm": (tm + d) % slices}

    x, zl = tm % xs, tm // xs

    def in_plane(dx, dy):
        return {"traj": place(0, dy) * 2 + core, "tm": zl * xs + (x + dx) % xs}

    plane = [(dx, dy) for dx in range(xs) for dy in range(side) if dx or dy]
    plane.sort(key=lambda d: -min(d[0], xs - d[0]) - min(d[1], side - d[1]))
    thick = vecs // xs
    share = pl.ds(pl.multiple_of(x * thick, thick), thick)

    hops = sorted(range(1, side), key=lambda d: -min(d, side - d))
    near_first = hops[::-1]
    barrier = pltpu.get_barrier_semaphore()
    for d in hops:
        pl.semaphore_signal(barrier, inc=1, device_id=at(place(d, 0)), device_id_type=MESH)
    for dx, dy in plane:
        if dy:
            pl.semaphore_signal(barrier, inc=1, device_id=in_plane(dx, dy), device_id_type=MESH)
    pl.semaphore_signal(barrier, inc=1, device_id=at(chip, 1), device_id_type=MESH)
    for d in range(1, slices):
        pl.semaphore_signal(barrier, inc=1, device_id=at_slice(d), device_id_type=MESH)

    reads = [
        pltpu.make_async_copy(src, dst, local_sem.at[k])
        for k, (src, dst) in enumerate(
            (
                (states.at[0], coords),
                (lists_in, lists),
                (counts_in, counts),
                (scale_in, scale),
                (vectors, ve_all.at[chip]),
            )
        )
    ]
    for read in reads:
        read.start()
    row_sum[...] = jnp.zeros_like(row_sum)
    total[...] = jnp.zeros_like(total)
    for read in reads:
        read.wait()
    slot = lax.broadcasted_iota(jnp.int32, (1, lists.shape[1]), 1)
    ls_all[chip] = jnp.full((1, 2 * half), NONE, jnp.int32)
    for b in range(blocks):
        ls_all[chip, :, b * half : b * half + lists.shape[1]] = jnp.where(
            slot < counts[b], lists[b : b + 1, :], NONE
        )
    st_all[chip] = jnp.round(coords[...] * STEP).astype(jnp.int32).astype(jnp.int16)
    basis[:, :own] = augmented(st_all[chip], -2.0, "hlhl", 3)
    rate = -math.log2(math.e) / (STEP * STEP) / scale[0]
    pl.semaphore_wait(barrier, (side - 1) + (xs * side - xs) + 1 + slices - 1)

    def copy(src, dst, send, recv, device):
        return pltpu.make_async_remote_copy(
            src_ref=src, dst_ref=dst, send_sem=send, recv_sem=recv, device_id=device, device_id_type=MESH
        )

    def send_z(everyone, send, recv, d):
        mine = everyone.at[chip]
        copy(mine, mine, send, recv.at[chip], at(place(d, 0))).start()

    def send_y(everyone, send, recv):
        mine = everyone.at[chip]
        for d in hops:
            copy(mine, mine, send, recv.at[chip], at(place(0, d))).start()

    def forward(everyone, send, recv, dz):
        theirs = everyone.at[place(dz, 0)]
        arrived = recv.at[place(dz, 0)]
        wait_for(theirs, arrived)
        for d in hops:
            copy(theirs, theirs, send, arrived, at(place(0, d))).start()

    def all_sent(everyone, send):
        every = everyone.at[pl.ds(0, chips - 1)]
        wait_for(every, send)

    def send_share(d):
        mine = ve_all.at[chip, share]
        copy(mine, mine, vz_send, vz_recv.at[zh], at(place(d, 0))).start()

    def forward_share(d):
        there = place(d, 0)
        theirs = ve_all.at[there, share]
        wait_for(theirs, vz_recv.at[(zh + d) % side])
        for dx, dy in plane:
            copy(theirs, theirs, ve_send.at[d], ve_recv.at[there], in_plane(dx, dy)).start()

    def shares_sent():
        wait_for(ve_all.at[pl.ds(0, side - 1), pl.ds(0, thick)], vz_send)
        wait_for(ve_all.at[pl.ds(0, side - 1)], ve_send.at[0])
        for d in hops:
            wait_for(ve_all.at[pl.ds(0, len(plane)), pl.ds(0, thick)], ve_send.at[d])

    def share_wait(dz, dy):
        where = place(dz, dy)
        if dy:
            wait_for(ve_all.at[where], ve_recv.at[where])
        elif dz and xs > 1:
            wait_for(ve_all.at[where, pl.ds(0, vecs - thick)], ve_recv.at[where])

    def shard_wait(dz, dy):
        where = place(dz, dy)
        if dy:
            wait_for(sc_all.at[where], sc_recv.at[where])

    def pair(src, dst, k):
        return copy(src, dst, pair_send.at[k], pair_recv.at[k], at(chip, 1))

    st = (st_all, st_send, st_recv)
    ls = (ls_all, ls_send, ls_recv)
    sc = (sc_all, sc_send, sc_recv)
    near, far = near_first[:-1], near_first[-1]
    first_steps = [(w, d) for w in ("st", "ls", "ve") for d in hops + [0]]
    for what, d in first_steps:
        group = {"st": st, "ls": ls, "ve": (ve_all, ve_send.at[0], ve_recv)}[what]
        if d:
            send_share(d) if what == "ve" else send_z(*group, d)
        else:
            send_y(*group)
        if what == "st" and not d:
            st_swap = pair(st_all.at[chip], st_pair, 0)
            ls_swap = pair(ls_all.at[chip], ls_pair, 1)
            st_swap.start()
            ls_swap.start()
    def build(where):
        base = 4 * where + 2 * core
        entry = lax.broadcasted_iota(jnp.int32, (8, 2 * half), 0)
        lane = lax.broadcasted_iota(jnp.int32, (8, 2 * half), 1)
        block = lane // half
        there = jnp.where(entry == block, jnp.broadcast_to(ls_all[where], (8, 2 * half)), NONE)
        for b in range(2 * blocks):
            held = ls_all[chip] if b < blocks else ls_pair[...]
            mine = jnp.where(block == b % blocks, jnp.broadcast_to(held, (8, 2 * half)), NONE)
            name = 4 * chip + 2 * ((core + b // blocks) % 2) + b % blocks
            lanes = slice(b * BLK, (b + 1) * BLK)
            for mask, hit in ((mask_1, mine == base + entry), (mask_2, there == name)):
                found = jnp.max(jnp.where(hit, 1.0, 0.0), axis=1, keepdims=True)
                mask[where, :, lanes] = jnp.broadcast_to(found, (8, BLK))
        rows = augmented(st_all[where], 1.0, "hhll", 0)
        for h in range(blocks):
            part = slice(h * BLK, (h + 1) * BLK)
            distance = lax.dot_general(
                rows[:, part],
                basis[...],
                (((0,), (0,)), ((), ())),
                preferred_element_type=jnp.float32,
            )
            weight = jnp.exp2(distance * rate)
            linked = weight * mask_1[where, h : h + 1, :]
            row_sum[...] += jnp.sum(linked.reshape(BLK // 8, 8, 2 * own), axis=0)
            first[where, part, :] = linked.astype(jnp.bfloat16)
            second[where, part, :] = (weight * mask_2[where, h : h + 1, :]).astype(jnp.bfloat16)

    def builds(dz):
        build(place(dz, 0))

        def body(dy, carry):
            where = place(dz, dy)
            wait_for(st_all.at[where], st_recv.at[where])
            wait_for(ls_all.at[where], ls_recv.at[where])
            build(where)
            return carry

        lax.fori_loop(1, side, body, 0)

    def products(everyone, arrive, weights, dz, cores=(1, 0), wait=True):
        for c in cores:
            part = slice(c * own, (c + 1) * own)
            sums = total[:, part]
            for dy in range(side):
                where = place(dz, dy)
                if wait and c == cores[0]:
                    arrive(dz, dy)
                sums = sums + jnp.dot(
                    everyone[where], weights[where, :, part], preferred_element_type=jnp.float32
                )
            total[:, part] = sums

    second_steps = [("fs", d) for d in near] + [("b0", 0), ("b", 0), ("fs", far)]
    second_steps += [("fv", d) for d in near] + [("b", d) for d in near[:1]] + [("fv", far)]
    second_steps += [("b", d) for d in near[1:]] + [("p", 0), ("b", far)] + [("p", d) for d in near]
    for step, dz in second_steps:
        if step == "fs":
            forward(*st, dz)
            forward(*ls, dz)
        elif step == "b0":
            st_swap.wait_recv()
            basis[:, own:] = augmented(st_pair[...], -2.0, "hlhl", 3)
            ls_swap.wait_recv()
        elif step == "b":
            builds(dz)
        elif step == "fv":
            forward_share(dz)
        elif step == "p":
            products(ve_all, share_wait, first, dz)

    products(ve_all, share_wait, first, far, (1,))
    px_out[0, :vecs] = total[:, own:]
    px_out[0, vecs:] = row_sum[:, own:]
    swap_1 = pair(px_out.at[0], px_in.at[0], 2)
    swap_1.start()
    products(ve_all, share_wait, first, far, (0,), False)
    swap_1.wait_recv()
    sums = jnp.sum(row_sum[:, :own] + px_in[0, vecs:], axis=0, keepdims=True)
    sc_all[chip] = ((total[:, :own] + px_in[0, :vecs]) / (sums * sums)).astype(jnp.bfloat16)
    @pl.when(zh == 0)
    def _first_group():
        for d in hops:
            send_z(*sc, d)

    @pl.when(zh > 0)
    def _to_first_group():
        send_z(*sc, side - zh)

    send_y(*sc)
    total[...] = jnp.zeros_like(total)
    products(sc_all, shard_wait, second, 0)

    @pl.when(zh > 0)
    def _to_others():
        for k in range(1, side - 1):
            send_z(*sc, (k + (k >= zh).astype(jnp.int32) - zh) % side)

    for dz in near:
        forward(*sc, dz)
    forward(*sc, far)
    for dz in near:
        products(sc_all, shard_wait, second, dz)
    products(sc_all, shard_wait, second, far, (1,))
    px_out[1, :vecs] = total[:, own:]
    swap_2 = pair(px_out.at[1, pl.ds(0, vecs)], px_in.at[1, pl.ds(0, vecs)], 3)
    swap_2.start()
    products(sc_all, shard_wait, second, far, (0,), False)
    swap_2.wait_recv()

    tiles = rs_out.shape[0]
    wide = own // 128
    per = tiles // slices
    for t in range(tiles):
        rows, lanes = slice(t // wide * 8, t // wide * 8 + 8), slice(t % wide * 128, t % wide * 128 + 128)
        rs_out[t] = total[rows, lanes] + px_in[1, rows, lanes]

    for d in range(1, slices):
        there = (tm + d) % slices
        copy(
            rs_out.at[pl.ds(there * per, per)], rs_in.at[tm], rs_send, rs_recv.at[tm], at_slice(d)
        ).start()

    def scattered(d, carry):
        there = (tm + d) % slices
        wait_for(rs_in.at[there], rs_recv.at[there])
        return carry

    rs_in[tm] = rs_out[pl.ds(tm * per, per)]
    lax.fori_loop(1, slices, scattered, 0)
    ag[tm] = jnp.sum(rs_in[...], axis=0)

    for d in range(1, slices):
        copy(ag.at[tm], ag.at[tm], ag_send, ag_recv.at[tm], at_slice(d)).start()

    def arrived(d, carry):
        there = (tm + d) % slices
        wait_for(ag.at[there], ag_recv.at[there])
        return carry

    lax.fori_loop(1, slices, arrived, 0)
    for t in range(tiles):
        rows, lanes = slice(t // wide * 8, t // wide * 8 + 8), slice(t % wide * 128, t % wide * 128 + 128)
        out[rows, lanes] = ag[t // per, t % per]

    all_sent(st_all, st_send)
    all_sent(ls_all, ls_send)
    shares_sent()
    all_sent(sc_all, sc_send)
    for swap in (st_swap, ls_swap, swap_1, swap_2):
        swap.wait_send()

    wait_for(rs_in.at[pl.ds(0, slices - 1)], rs_send)
    wait_for(ag.at[pl.ds(0, slices - 1)], ag_send)


def per_device(side, xs, slices, states, vectors, kernel_scale, neighbour_blocks, neighbour_count):
    coords, own = states.shape[1:]
    vecs = vectors.shape[0]
    chips = side * side
    tiles = vecs * own // 1024
    vmem = pl.BlockSpec(memory_space=pltpu.VMEM)
    hbm = pl.BlockSpec(memory_space=pltpu.HBM)
    dma = pltpu.SemaphoreType.DMA
    return pl.pallas_call(
        functools.partial(kernel, side, xs, slices),
        out_shape=pltpu.VMEM((vecs, own), jnp.float32),
        in_specs=[hbm] * 5,
        out_specs=vmem,
        scratch_shapes=[
            pltpu.VMEM((coords, own), jnp.float32),
            pltpu.SMEM((1,), jnp.float32),
            pltpu.VMEM(neighbour_blocks.shape, jnp.int32),
            pltpu.SMEM(neighbour_count.shape, jnp.int32),
            pltpu.VMEM((chips, coords, own), jnp.int16),
            pltpu.VMEM((coords, own), jnp.int16),
            pltpu.VMEM((chips, 1, 128), jnp.int32),
            pltpu.VMEM((1, 128), jnp.int32),
            pltpu.VMEM((chips, vecs, own), jnp.bfloat16),
            pltpu.VMEM((chips, vecs, own), jnp.bfloat16),
            pltpu.VMEM((4 * coords + 16, 2 * own), jnp.bfloat16),
            pltpu.VMEM((chips, 8, 2 * own), jnp.float32),
            pltpu.VMEM((chips, 8, 2 * own), jnp.float32),
            pltpu.VMEM((chips, own, 2 * own), jnp.bfloat16),
            pltpu.VMEM((chips, own, 2 * own), jnp.bfloat16),
            pltpu.VMEM((8, 2 * own), jnp.float32),
            pltpu.VMEM((vecs, 2 * own), jnp.float32),
            pltpu.VMEM((2, vecs + 8, own), jnp.float32),
            pltpu.VMEM((2, vecs + 8, own), jnp.float32),
            pltpu.VMEM((tiles, 8, 128), jnp.float32),
            pltpu.VMEM((slices, tiles // slices, 8, 128), jnp.float32),
            pltpu.VMEM((slices, tiles // slices, 8, 128), jnp.float32),
            dma,
            dma((chips,)),
            dma,
            dma((chips,)),
            dma,
            dma((side,)),
            dma((side,)),
            dma((chips,)),
            dma,
            dma((chips,)),
            dma((4,)),
            dma((4,)),
            dma,
            dma((slices,)),
            dma,
            dma((slices,)),
            dma((5,)),
        ],
        compiler_params=pltpu.CompilerParams(
            collective_id=0, has_side_effects=True, vmem_limit_bytes=VMEM_KIB * 1024
        ),
    )(states, vectors, kernel_scale, neighbour_blocks, neighbour_count)


def solution(mesh):
    side, slices = math.isqrt(mesh.shape["traj"] // 2), mesh.shape["tm"]
    xs = min(side, slices)
    return jax.shard_map(
        functools.partial(per_device, side, xs, slices),
        mesh=mesh,
        in_specs=(P("tm", None, "traj"), P(None, "traj"), P("tm"), P("traj", None), P("traj")),
        out_specs=P(None, "traj"),
        check_vma=False,
    )
```

```python
import functools
import math

import jax
import jax.numpy as jnp
from jax import lax
from jax.experimental import pallas as pl
from jax.experimental.pallas import tpu as pltpu
from jax.sharding import PartitionSpec as P

MESH = pl.DeviceIdType.MESH
BLK = 128
VMEM_KIB = 55170
STEP = 5461.0
NONE = -1


def wait_for(ref, sem):
    pltpu.make_async_copy(ref, ref, sem).wait()


def digits(codes):
    high = (codes + 128) >> 8
    low = codes - (high << 8)
    return (high << 8).astype(jnp.float32), low.astype(jnp.float32)


def three_parts(value):
    one = value.astype(jnp.bfloat16).astype(jnp.float32)
    two = (value - one).astype(jnp.bfloat16).astype(jnp.float32)
    return one, two, value - one - two


def augmented(codes, times, order, first):
    whole = codes.astype(jnp.int32)
    high, low = digits(whole)
    real = whole.astype(jnp.float32)
    square = jnp.sum(real * real, axis=0, keepdims=True)
    row = lax.broadcasted_iota(jnp.int32, (16, codes.shape[1]), 0)
    extra = jnp.where((row >= 3 - first) & (row < 6 - first), 1.0, 0.0)
    for k, part in enumerate(three_parts(square)):
        extra = jnp.where(row == first + k, part, extra)
    both = {"h": (high * times).astype(jnp.bfloat16), "l": (low * times).astype(jnp.bfloat16)}
    return jnp.concatenate([both[k] for k in order] + [extra.astype(jnp.bfloat16)], axis=0)


def kernel(
    side,
    xs,
    slices,
    states,
    vectors,
    scale_in,
    lists_in,
    counts_in,
    out,
    coords,
    scale,
    lists,
    counts,
    st_all,
    st_pair,
    ls_all,
    ls_pair,
    ve_all,
    sc_all,
    basis,
    mask_1,
    mask_2,
    first,
    second,
    row_sum,
    total,
    px_out,
    px_in,
    rs_out,
    rs_in,
    ag,
    st_send,
    st_recv,
    ls_send,
    ls_recv,
    vz_send,
    vz_recv,
    ve_send,
    ve_recv,
    sc_send,
    sc_recv,
    pair_send,
    pair_recv,
    rs_send,
    rs_recv,
    ag_send,
    ag_recv,
    local_sem,
):
    chips = side * side
    traj, tm = lax.axis_index("traj"), lax.axis_index("tm")
    core, chip = traj % 2, traj // 2
    y, zh = chip % side, chip // side
    own = states.shape[2]
    vecs = vectors.shape[0]
    half = ls_pair.shape[1] // 2
    blocks = own // BLK

    def place(dz, dy):
        return ((zh + dz) % side) * side + (y + dy) % side

    def at(where, other=0):
        return {"traj": where * 2 + (core + other) % 2, "tm": tm}

    def at_slice(d):
        return {"traj": traj, "tm": (tm + d) % slices}

    x, zl = tm % xs, tm // xs

    def in_plane(dx, dy):
        return {"traj": place(0, dy) * 2 + core, "tm": zl * xs + (x + dx) % xs}

    plane = [(dx, dy) for dx in range(xs) for dy in range(side) if dx or dy]
    plane.sort(key=lambda d: -min(d[0], xs - d[0]) - min(d[1], side - d[1]))
    thick = vecs // xs
    share = pl.ds(pl.multiple_of(x * thick, thick), thick)

    hops = sorted(range(1, side), key=lambda d: -min(d, side - d))
    near_first = hops[::-1]
    barrier = pltpu.get_barrier_semaphore()
    for d in hops:
        pl.semaphore_signal(barrier, inc=1, device_id=at(place(d, 0)), device_id_type=MESH)
    for dx, dy in plane:
        if dy:
            pl.semaphore_signal(barrier, inc=1, device_id=in_plane(dx, dy), device_id_type=MESH)
    pl.semaphore_signal(barrier, inc=1, device_id=at(chip, 1), device_id_type=MESH)
    for d in range(1, slices):
        pl.semaphore_signal(barrier, inc=1, device_id=at_slice(d), device_id_type=MESH)

    reads = [
        pltpu.make_async_copy(src, dst, local_sem.at[k])
        for k, (src, dst) in enumerate(
            (
                (states.at[0], coords),
                (lists_in, lists),
                (counts_in, counts),
                (scale_in, scale),
                (vectors, ve_all.at[chip]),
            )
        )
    ]
    for read in reads:
        read.start()
    row_sum[...] = jnp.zeros_like(row_sum)
    total[...] = jnp.zeros_like(total)
    for read in reads:
        read.wait()
    slot = lax.broadcasted_iota(jnp.int32, (1, lists.shape[1]), 1)
    ls_all[chip] = jnp.full((1, 2 * half), NONE, jnp.int32)
    for b in range(blocks):
        ls_all[chip, :, b * half : b * half + lists.shape[1]] = jnp.where(
            slot < counts[b], lists[b : b + 1, :], NONE
        )
    st_all[chip] = jnp.round(coords[...] * STEP).astype(jnp.int32).astype(jnp.int16)
    basis[:, :own] = augmented(st_all[chip], -2.0, "hlhl", 3)
    rate = -math.log2(math.e) / (STEP * STEP) / scale[0]
    pl.semaphore_wait(barrier, (side - 1) + (xs * side - xs) + 1 + slices - 1)

    def copy(src, dst, send, recv, device):
        return pltpu.make_async_remote_copy(
            src_ref=src, dst_ref=dst, send_sem=send, recv_sem=recv, device_id=device, device_id_type=MESH
        )

    def send_z(everyone, send, recv, d):
        mine = everyone.at[chip]
        copy(mine, mine, send, recv.at[chip], at(place(d, 0))).start()

    def send_y(everyone, send, recv):
        mine = everyone.at[chip]
        for d in hops:
            copy(mine, mine, send, recv.at[chip], at(place(0, d))).start()

    def forward(everyone, send, recv, dz):
        theirs = everyone.at[place(dz, 0)]
        arrived = recv.at[place(dz, 0)]
        wait_for(theirs, arrived)
        for d in hops:
            copy(theirs, theirs, send, arrived, at(place(0, d))).start()

    def all_sent(everyone, send):
        every = everyone.at[pl.ds(0, chips - 1)]
        wait_for(every, send)

    def send_share(d):
        mine = ve_all.at[chip, share]
        copy(mine, mine, vz_send, vz_recv.at[zh], at(place(d, 0))).start()

    def forward_share(d):
        there = place(d, 0)
        theirs = ve_all.at[there, share]
        wait_for(theirs, vz_recv.at[(zh + d) % side])
        for dx, dy in plane:
            copy(theirs, theirs, ve_send.at[d], ve_recv.at[there], in_plane(dx, dy)).start()

    def shares_sent():
        wait_for(ve_all.at[pl.ds(0, side - 1), pl.ds(0, thick)], vz_send)
        wait_for(ve_all.at[pl.ds(0, side - 1)], ve_send.at[0])
        for d in hops:
            wait_for(ve_all.at[pl.ds(0, len(plane)), pl.ds(0, thick)], ve_send.at[d])

    def share_wait(dz, dy):
        where = place(dz, dy)
        if dy:
            wait_for(ve_all.at[where], ve_recv.at[where])
        elif dz and xs > 1:
            wait_for(ve_all.at[where, pl.ds(0, vecs - thick)], ve_recv.at[where])

    def shard_wait(dz, dy):
        where = place(dz, dy)
        if dy:
            wait_for(sc_all.at[where], sc_recv.at[where])

    def pair(src, dst, k):
        return copy(src, dst, pair_send.at[k], pair_recv.at[k], at(chip, 1))

    st = (st_all, st_send, st_recv)
    ls = (ls_all, ls_send, ls_recv)
    sc = (sc_all, sc_send, sc_recv)
    near, far = near_first[:-1], near_first[-1]
    first_steps = [(w, d) for w in ("st", "ls", "ve") for d in hops + [0]]
    for what, d in first_steps:
        group = {"st": st, "ls": ls, "ve": (ve_all, ve_send.at[0], ve_recv)}[what]
        if d:
            send_share(d) if what == "ve" else send_z(*group, d)
        else:
            send_y(*group)
        if what == "st" and not d:
            st_swap = pair(st_all.at[chip], st_pair, 0)
            ls_swap = pair(ls_all.at[chip], ls_pair, 1)
            st_swap.start()
            ls_swap.start()
    def build(where):
        base = 4 * where + 2 * core
        entry = lax.broadcasted_iota(jnp.int32, (8, 2 * half), 0)
        lane = lax.broadcasted_iota(jnp.int32, (8, 2 * half), 1)
        block = lane // half
        there = jnp.where(entry == block, jnp.broadcast_to(ls_all[where], (8, 2 * half)), NONE)
        for b in range(2 * blocks):
            held = ls_all[chip] if b < blocks else ls_pair[...]
            mine = jnp.where(block == b % blocks, jnp.broadcast_to(held, (8, 2 * half)), NONE)
            name = 4 * chip + 2 * ((core + b // blocks) % 2) + b % blocks
            lanes = slice(b * BLK, (b + 1) * BLK)
            for mask, hit in ((mask_1, mine == base + entry), (mask_2, there == name)):
                found = jnp.max(jnp.where(hit, 1.0, 0.0), axis=1, keepdims=True)
                mask[where, :, lanes] = jnp.broadcast_to(found, (8, BLK))
        rows = augmented(st_all[where], 1.0, "hhll", 0)
        for h in range(blocks):
            part = slice(h * BLK, (h + 1) * BLK)
            distance = lax.dot_general(
                rows[:, part],
                basis[...],
                (((0,), (0,)), ((), ())),
                preferred_element_type=jnp.float32,
            )
            weight = jnp.exp2(distance * rate)
            linked = weight * mask_1[where, h : h + 1, :]
            row_sum[...] += jnp.sum(linked.reshape(BLK // 8, 8, 2 * own), axis=0)
            first[where, part, :] = linked.astype(jnp.bfloat16)
            second[where, part, :] = (weight * mask_2[where, h : h + 1, :]).astype(jnp.bfloat16)

    def builds(dz):
        build(place(dz, 0))

        def body(dy, carry):
            where = place(dz, dy)
            wait_for(st_all.at[where], st_recv.at[where])
            wait_for(ls_all.at[where], ls_recv.at[where])
            build(where)
            return carry

        lax.fori_loop(1, side, body, 0)

    def products(everyone, arrive, weights, dz, cores=(1, 0), wait=True):
        for c in cores:
            part = slice(c * own, (c + 1) * own)
            sums = total[:, part]
            for dy in range(side):
                where = place(dz, dy)
                if wait and c == cores[0]:
                    arrive(dz, dy)
                sums = sums + jnp.dot(
                    everyone[where], weights[where, :, part], preferred_element_type=jnp.float32
                )
            total[:, part] = sums

    second_steps = [("fs", d) for d in near] + [("b0", 0), ("b", 0), ("fs", far)]
    second_steps += [("fv", d) for d in near] + [("b", d) for d in near[:1]] + [("fv", far)]
    second_steps += [("b", d) for d in near[1:]] + [("p", 0), ("b", far)] + [("p", d) for d in near]
    for step, dz in second_steps:
        if step == "fs":
            forward(*st, dz)
            forward(*ls, dz)
        elif step == "b0":
            st_swap.wait_recv()
            basis[:, own:] = augmented(st_pair[...], -2.0, "hlhl", 3)
            ls_swap.wait_recv()
        elif step == "b":
            builds(dz)
        elif step == "fv":
            forward_share(dz)
        elif step == "p":
            products(ve_all, share_wait, first, dz)

    products(ve_all, share_wait, first, far, (1,))
    px_out[0, :vecs] = total[:, own:]
    px_out[0, vecs:] = row_sum[:, own:]
    swap_1 = pair(px_out.at[0], px_in.at[0], 2)
    swap_1.start()
    products(ve_all, share_wait, first, far, (0,), False)
    swap_1.wait_recv()
    sums = jnp.sum(row_sum[:, :own] + px_in[0, vecs:], axis=0, keepdims=True)
    sc_all[chip] = ((total[:, :own] + px_in[0, :vecs]) / (sums * sums)).astype(jnp.bfloat16)
    @pl.when(zh == 0)
    def _first_group():
        for d in hops:
            send_z(*sc, d)

    @pl.when(zh > 0)
    def _to_first_group():
        send_z(*sc, side - zh)

    send_y(*sc)
    total[...] = jnp.zeros_like(total)
    products(sc_all, shard_wait, second, 0)

    @pl.when(zh > 0)
    def _to_others():
        for k in range(1, side - 1):
            send_z(*sc, (k + (k >= zh).astype(jnp.int32) - zh) % side)

    for dz in near:
        forward(*sc, dz)
    forward(*sc, far)
    for dz in near:
        products(sc_all, shard_wait, second, dz)
    products(sc_all, shard_wait, second, far, (1,))
    px_out[1, :vecs] = total[:, own:]
    swap_2 = pair(px_out.at[1, pl.ds(0, vecs)], px_in.at[1, pl.ds(0, vecs)], 3)
    swap_2.start()
    products(sc_all, shard_wait, second, far, (0,), False)
    swap_2.wait_recv()

    tiles = rs_out.shape[0]
    wide = own // 128
    per = tiles // slices
    for t in range(tiles):
        rows, lanes = slice(t // wide * 8, t // wide * 8 + 8), slice(t % wide * 128, t % wide * 128 + 128)
        rs_out[t] = total[rows, lanes] + px_in[1, rows, lanes]

    def scatter(there):
        copy(
            rs_out.at[pl.ds(there * per, per)],
            rs_in.at[tm],
            rs_send,
            rs_recv.at[tm],
            {"traj": traj, "tm": there},
        ).start()

    def far_first(send):
        runs = slices // xs
        across = sorted(range(xs), key=lambda d: -min(d, xs - d))
        for k in range(runs):
            run = jnp.where(2 * zl >= runs, k, runs - 1 - k)
            for d in across:
                there = run * xs + (x + d) % xs
                if d:
                    send(there)
                else:
                    pl.when(run != zl)(functools.partial(send, there))

    far_first(scatter)

    def scattered(d, carry):
        there = (tm + d) % slices
        wait_for(rs_in.at[there], rs_recv.at[there])
        return carry

    rs_in[tm] = rs_out[pl.ds(tm * per, per)]
    lax.fori_loop(1, slices, scattered, 0)
    ag[tm] = jnp.sum(rs_in[...], axis=0)

    def spread(there):
        copy(
            ag.at[tm], ag.at[tm], ag_send, ag_recv.at[tm], {"traj": traj, "tm": there}
        ).start()

    far_first(spread)

    def arrived(d, carry):
        there = (tm + d) % slices
        wait_for(ag.at[there], ag_recv.at[there])
        return carry

    lax.fori_loop(1, slices, arrived, 0)
    for t in range(tiles):
        rows, lanes = slice(t // wide * 8, t // wide * 8 + 8), slice(t % wide * 128, t % wide * 128 + 128)
        out[rows, lanes] = ag[t // per, t % per]

    all_sent(st_all, st_send)
    all_sent(ls_all, ls_send)
    shares_sent()
    all_sent(sc_all, sc_send)
    for swap in (st_swap, ls_swap, swap_1, swap_2):
        swap.wait_send()

    wait_for(rs_in.at[pl.ds(0, slices - 1)], rs_send)
    wait_for(ag.at[pl.ds(0, slices - 1)], ag_send)


def per_device(side, xs, slices, states, vectors, kernel_scale, neighbour_blocks, neighbour_count):
    coords, own = states.shape[1:]
    vecs = vectors.shape[0]
    chips = side * side
    tiles = vecs * own // 1024
    vmem = pl.BlockSpec(memory_space=pltpu.VMEM)
    hbm = pl.BlockSpec(memory_space=pltpu.HBM)
    dma = pltpu.SemaphoreType.DMA
    return pl.pallas_call(
        functools.partial(kernel, side, xs, slices),
        out_shape=pltpu.VMEM((vecs, own), jnp.float32),
        in_specs=[hbm] * 5,
        out_specs=vmem,
        scratch_shapes=[
            pltpu.VMEM((coords, own), jnp.float32),
            pltpu.SMEM((1,), jnp.float32),
            pltpu.VMEM(neighbour_blocks.shape, jnp.int32),
            pltpu.SMEM(neighbour_count.shape, jnp.int32),
            pltpu.VMEM((chips, coords, own), jnp.int16),
            pltpu.VMEM((coords, own), jnp.int16),
            pltpu.VMEM((chips, 1, 128), jnp.int32),
            pltpu.VMEM((1, 128), jnp.int32),
            pltpu.VMEM((chips, vecs, own), jnp.bfloat16),
            pltpu.VMEM((chips, vecs, own), jnp.bfloat16),
            pltpu.VMEM((4 * coords + 16, 2 * own), jnp.bfloat16),
            pltpu.VMEM((chips, 8, 2 * own), jnp.float32),
            pltpu.VMEM((chips, 8, 2 * own), jnp.float32),
            pltpu.VMEM((chips, own, 2 * own), jnp.bfloat16),
            pltpu.VMEM((chips, own, 2 * own), jnp.bfloat16),
            pltpu.VMEM((8, 2 * own), jnp.float32),
            pltpu.VMEM((vecs, 2 * own), jnp.float32),
            pltpu.VMEM((2, vecs + 8, own), jnp.float32),
            pltpu.VMEM((2, vecs + 8, own), jnp.float32),
            pltpu.VMEM((tiles, 8, 128), jnp.float32),
            pltpu.VMEM((slices, tiles // slices, 8, 128), jnp.float32),
            pltpu.VMEM((slices, tiles // slices, 8, 128), jnp.float32),
            dma,
            dma((chips,)),
            dma,
            dma((chips,)),
            dma,
            dma((side,)),
            dma((side,)),
            dma((chips,)),
            dma,
            dma((chips,)),
            dma((4,)),
            dma((4,)),
            dma,
            dma((slices,)),
            dma,
            dma((slices,)),
            dma((5,)),
        ],
        compiler_params=pltpu.CompilerParams(
            collective_id=0, has_side_effects=True, vmem_limit_bytes=VMEM_KIB * 1024
        ),
    )(states, vectors, kernel_scale, neighbour_blocks, neighbour_count)


def solution(mesh):
    side, slices = math.isqrt(mesh.shape["traj"] // 2), mesh.shape["tm"]
    xs = min(side, slices)
    return jax.shard_map(
        functools.partial(per_device, side, xs, slices),
        mesh=mesh,
        in_specs=(P("tm", None, "traj"), P(None, "traj"), P("tm"), P("traj", None), P("traj")),
        out_specs=P(None, "traj"),
        check_vma=False,
    )
```

```python
import functools
import math

import jax
import jax.numpy as jnp
from jax import lax
from jax.experimental import pallas as pl
from jax.experimental.pallas import tpu as pltpu
from jax.sharding import PartitionSpec as P

MESH = pl.DeviceIdType.MESH
BLK = 128
VMEM_KIB = 55170
STEP = 5461.0
NONE = -1


def wait_for(ref, sem):
    pltpu.make_async_copy(ref, ref, sem).wait()


def digits(codes):
    high = (codes + 128) >> 8
    low = codes - (high << 8)
    return (high << 8).astype(jnp.float32), low.astype(jnp.float32)


def three_parts(value):
    one = value.astype(jnp.bfloat16).astype(jnp.float32)
    two = (value - one).astype(jnp.bfloat16).astype(jnp.float32)
    return one, two, value - one - two


def augmented(codes, times, order, first):
    whole = codes.astype(jnp.int32)
    high, low = digits(whole)
    real = whole.astype(jnp.float32)
    square = jnp.sum(real * real, axis=0, keepdims=True)
    row = lax.broadcasted_iota(jnp.int32, (16, codes.shape[1]), 0)
    extra = jnp.where((row >= 3 - first) & (row < 6 - first), 1.0, 0.0)
    for k, part in enumerate(three_parts(square)):
        extra = jnp.where(row == first + k, part, extra)
    both = {"h": (high * times).astype(jnp.bfloat16), "l": (low * times).astype(jnp.bfloat16)}
    return jnp.concatenate([both[k] for k in order] + [extra.astype(jnp.bfloat16)], axis=0)


def kernel(
    side,
    xs,
    slices,
    states,
    vectors,
    scale_in,
    lists_in,
    counts_in,
    out,
    coords,
    scale,
    lists,
    counts,
    st_all,
    st_pair,
    ls_all,
    ls_pair,
    ve_all,
    sc_all,
    basis,
    mask_1,
    mask_2,
    first,
    second,
    row_sum,
    total,
    px_out,
    px_in,
    rs_out,
    rs_in,
    ag,
    st_send,
    st_recv,
    ls_send,
    ls_recv,
    vz_send,
    vz_recv,
    ve_send,
    ve_recv,
    sc_send,
    sc_recv,
    pair_send,
    pair_recv,
    rs_send,
    rs_recv,
    ag_send,
    ag_recv,
    local_sem,
):
    chips = side * side
    traj, tm = lax.axis_index("traj"), lax.axis_index("tm")
    core, chip = traj % 2, traj // 2
    y, zh = chip % side, chip // side
    own = states.shape[2]
    vecs = vectors.shape[0]
    half = ls_pair.shape[1] // 2
    blocks = own // BLK

    def place(dz, dy):
        return ((zh + dz) % side) * side + (y + dy) % side

    def at(where, other=0):
        return {"traj": where * 2 + (core + other) % 2, "tm": tm}

    def at_slice(d):
        return {"traj": traj, "tm": (tm + d) % slices}

    x, zl = tm % xs, tm // xs

    def in_plane(dx, dy):
        return {"traj": place(0, dy) * 2 + core, "tm": zl * xs + (x + dx) % xs}

    plane = [(dx, dy) for dx in range(xs) for dy in range(side) if dx or dy]
    plane.sort(key=lambda d: -min(d[0], xs - d[0]) - min(d[1], side - d[1]))
    thick = vecs // xs
    share = pl.ds(pl.multiple_of(x * thick, thick), thick)

    hops = sorted(range(1, side), key=lambda d: -min(d, side - d))
    near_first = hops[::-1]
    barrier = pltpu.get_barrier_semaphore()
    for d in hops:
        pl.semaphore_signal(barrier, inc=1, device_id=at(place(d, 0)), device_id_type=MESH)
    for dx, dy in plane:
        if dy:
            pl.semaphore_signal(barrier, inc=1, device_id=in_plane(dx, dy), device_id_type=MESH)
    pl.semaphore_signal(barrier, inc=1, device_id=at(chip, 1), device_id_type=MESH)
    for d in range(1, slices):
        pl.semaphore_signal(barrier, inc=1, device_id=at_slice(d), device_id_type=MESH)

    reads = [
        pltpu.make_async_copy(src, dst, local_sem.at[k])
        for k, (src, dst) in enumerate(
            (
                (states.at[0], coords),
                (lists_in, lists),
                (counts_in, counts),
                (scale_in, scale),
                (vectors, ve_all.at[chip]),
            )
        )
    ]
    for read in reads:
        read.start()
    row_sum[...] = jnp.zeros_like(row_sum)
    total[...] = jnp.zeros_like(total)
    for read in reads:
        read.wait()
    slot = lax.broadcasted_iota(jnp.int32, (1, lists.shape[1]), 1)
    ls_all[chip] = jnp.full((1, 2 * half), NONE, jnp.int32)
    for b in range(blocks):
        ls_all[chip, :, b * half : b * half + lists.shape[1]] = jnp.where(
            slot < counts[b], lists[b : b + 1, :], NONE
        )
    st_all[chip] = jnp.round(coords[...] * STEP).astype(jnp.int32).astype(jnp.int16)
    basis[:, :own] = augmented(st_all[chip], -2.0, "hlhl", 3)
    rate = -math.log2(math.e) / (STEP * STEP) / scale[0]
    pl.semaphore_wait(barrier, (side - 1) + (xs * side - xs) + 1 + slices - 1)

    def copy(src, dst, send, recv, device):
        return pltpu.make_async_remote_copy(
            src_ref=src, dst_ref=dst, send_sem=send, recv_sem=recv, device_id=device, device_id_type=MESH
        )

    def send_z(everyone, send, recv, d):
        mine = everyone.at[chip]
        copy(mine, mine, send, recv.at[chip], at(place(d, 0))).start()

    def send_y(everyone, send, recv):
        mine = everyone.at[chip]
        for d in hops:
            copy(mine, mine, send, recv.at[chip], at(place(0, d))).start()

    def forward(everyone, send, recv, dz):
        theirs = everyone.at[place(dz, 0)]
        arrived = recv.at[place(dz, 0)]
        wait_for(theirs, arrived)
        for d in hops:
            copy(theirs, theirs, send, arrived, at(place(0, d))).start()

    def all_sent(everyone, send):
        every = everyone.at[pl.ds(0, chips - 1)]
        wait_for(every, send)

    def send_share(d):
        mine = ve_all.at[chip, share]
        copy(mine, mine, vz_send, vz_recv.at[zh], at(place(d, 0))).start()

    def forward_share(d):
        there = place(d, 0)
        theirs = ve_all.at[there, share]
        wait_for(theirs, vz_recv.at[(zh + d) % side])
        for dx, dy in plane:
            copy(theirs, theirs, ve_send.at[d], ve_recv.at[there], in_plane(dx, dy)).start()

    def shares_sent():
        wait_for(ve_all.at[pl.ds(0, side - 1), pl.ds(0, thick)], vz_send)
        wait_for(ve_all.at[pl.ds(0, side - 1)], ve_send.at[0])
        for d in hops:
            wait_for(ve_all.at[pl.ds(0, len(plane)), pl.ds(0, thick)], ve_send.at[d])

    def share_wait(dz, dy):
        where = place(dz, dy)
        if dy:
            wait_for(ve_all.at[where], ve_recv.at[where])
        elif dz and xs > 1:
            wait_for(ve_all.at[where, pl.ds(0, vecs - thick)], ve_recv.at[where])

    def shard_wait(dz, dy):
        where = place(dz, dy)
        if dy:
            wait_for(sc_all.at[where], sc_recv.at[where])

    def pair(src, dst, k):
        return copy(src, dst, pair_send.at[k], pair_recv.at[k], at(chip, 1))

    st = (st_all, st_send, st_recv)
    ls = (ls_all, ls_send, ls_recv)
    sc = (sc_all, sc_send, sc_recv)
    near, far = near_first[:-1], near_first[-1]
    first_steps = [(w, d) for w in ("st", "ls", "ve") for d in hops + [0]]
    for what, d in first_steps:
        group = {"st": st, "ls": ls, "ve": (ve_all, ve_send.at[0], ve_recv)}[what]
        if d:
            send_share(d) if what == "ve" else send_z(*group, d)
        else:
            send_y(*group)
        if what == "st" and not d:
            st_swap = pair(st_all.at[chip], st_pair, 0)
            ls_swap = pair(ls_all.at[chip], ls_pair, 1)
            st_swap.start()
            ls_swap.start()
    def build(where):
        base = 4 * where + 2 * core
        entry = lax.broadcasted_iota(jnp.int32, (8, 2 * half), 0)
        lane = lax.broadcasted_iota(jnp.int32, (8, 2 * half), 1)
        block = lane // half
        there = jnp.where(entry == block, jnp.broadcast_to(ls_all[where], (8, 2 * half)), NONE)
        for b in range(2 * blocks):
            held = ls_all[chip] if b < blocks else ls_pair[...]
            mine = jnp.where(block == b % blocks, jnp.broadcast_to(held, (8, 2 * half)), NONE)
            name = 4 * chip + 2 * ((core + b // blocks) % 2) + b % blocks
            lanes = slice(b * BLK, (b + 1) * BLK)
            for mask, hit in ((mask_1, mine == base + entry), (mask_2, there == name)):
                found = jnp.max(jnp.where(hit, 1.0, 0.0), axis=1, keepdims=True)
                mask[where, :, lanes] = jnp.broadcast_to(found, (8, BLK))
        rows = augmented(st_all[where], 1.0, "hhll", 0)
        for h in range(blocks):
            part = slice(h * BLK, (h + 1) * BLK)
            distance = lax.dot_general(
                rows[:, part],
                basis[...],
                (((0,), (0,)), ((), ())),
                preferred_element_type=jnp.float32,
            )
            weight = jnp.exp2(distance * rate)
            linked = weight * mask_1[where, h : h + 1, :]
            row_sum[...] += jnp.sum(linked.reshape(BLK // 8, 8, 2 * own), axis=0)
            first[where, part, :] = linked.astype(jnp.bfloat16)
            second[where, part, :] = (weight * mask_2[where, h : h + 1, :]).astype(jnp.bfloat16)

    def builds(dz):
        build(place(dz, 0))

        def body(dy, carry):
            where = place(dz, dy)
            wait_for(st_all.at[where], st_recv.at[where])
            wait_for(ls_all.at[where], ls_recv.at[where])
            build(where)
            return carry

        lax.fori_loop(1, side, body, 0)

    def products(everyone, arrive, weights, dz, cores=(1, 0), wait=True):
        for c in cores:
            part = slice(c * own, (c + 1) * own)
            sums = total[:, part]
            for dy in range(side):
                where = place(dz, dy)
                if wait and c == cores[0]:
                    arrive(dz, dy)
                sums = sums + jnp.dot(
                    everyone[where], weights[where, :, part], preferred_element_type=jnp.float32
                )
            total[:, part] = sums

    second_steps = [("fs", d) for d in near] + [("b0", 0), ("b", 0), ("fs", far)]
    second_steps += [("fv", d) for d in near] + [("b", d) for d in near[:1]] + [("fv", far)]
    second_steps += [("b", d) for d in near[1:]] + [("p", 0), ("b", far)] + [("p", d) for d in near]
    for step, dz in second_steps:
        if step == "fs":
            forward(*st, dz)
            forward(*ls, dz)
        elif step == "b0":
            st_swap.wait_recv()
            basis[:, own:] = augmented(st_pair[...], -2.0, "hlhl", 3)
            ls_swap.wait_recv()
        elif step == "b":
            builds(dz)
        elif step == "fv":
            forward_share(dz)
        elif step == "p":
            products(ve_all, share_wait, first, dz)

    products(ve_all, share_wait, first, far, (1,))
    px_out[0, :vecs] = total[:, own:]
    px_out[0, vecs:] = row_sum[:, own:]
    swap_1 = pair(px_out.at[0], px_in.at[0], 2)
    swap_1.start()
    products(ve_all, share_wait, first, far, (0,), False)
    swap_1.wait_recv()
    sums = jnp.sum(row_sum[:, :own] + px_in[0, vecs:], axis=0, keepdims=True)
    sc_all[chip] = ((total[:, :own] + px_in[0, :vecs]) / (sums * sums)).astype(jnp.bfloat16)
    @pl.when(zh == 0)
    def _first_group():
        for d in hops:
            send_z(*sc, d)

    @pl.when(zh > 0)
    def _to_first_group():
        send_z(*sc, side - zh)

    send_y(*sc)
    total[...] = jnp.zeros_like(total)
    products(sc_all, shard_wait, second, 0)

    @pl.when(zh > 0)
    def _to_others():
        for k in range(1, side - 1):
            send_z(*sc, (k + (k >= zh).astype(jnp.int32) - zh) % side)

    for dz in near:
        forward(*sc, dz)
    forward(*sc, far)
    for dz in near:
        products(sc_all, shard_wait, second, dz)
    products(sc_all, shard_wait, second, far, (1,))
    px_out[1, :vecs] = total[:, own:]
    swap_2 = pair(px_out.at[1, pl.ds(0, vecs)], px_in.at[1, pl.ds(0, vecs)], 3)
    swap_2.start()
    products(sc_all, shard_wait, second, far, (0,), False)
    swap_2.wait_recv()

    tiles = rs_out.shape[0]
    wide = own // 128
    per = tiles // slices
    for t in range(tiles):
        rows, lanes = slice(t // wide * 8, t // wide * 8 + 8), slice(t % wide * 128, t % wide * 128 + 128)
        rs_out[t] = total[rows, lanes] + px_in[1, rows, lanes]

    def scatter(there):
        copy(
            rs_out.at[pl.ds(there * per, per)],
            rs_in.at[tm],
            rs_send,
            rs_recv.at[tm],
            {"traj": traj, "tm": there},
        ).start()

    def far_first(send):
        runs = slices // xs
        across = sorted(range(xs), key=lambda d: -min(d, xs - d))
        for k in range(runs):
            run = jnp.where(2 * zl >= runs, k, runs - 1 - k)
            for d in across:
                there = run * xs + (x + d) % xs
                if d:
                    send(there)
                else:
                    pl.when(run != zl)(functools.partial(send, there))

    far_first(scatter)

    def scattered(d, carry):
        there = (tm + d) % slices
        wait_for(rs_in.at[there], rs_recv.at[there])
        return carry

    rs_in[tm] = rs_out[pl.ds(tm * per, per)]
    lax.fori_loop(1, slices, scattered, 0)
    ag[tm] = jnp.sum(rs_in[...], axis=0)

    def spread(there):
        copy(
            ag.at[tm], ag.at[tm], ag_send, ag_recv.at[tm], {"traj": traj, "tm": there}
        ).start()

    far_first(spread)
    all_sent(st_all, st_send)
    all_sent(ls_all, ls_send)
    shares_sent()
    all_sent(sc_all, sc_send)
    for swap in (st_swap, ls_swap, swap_1, swap_2):
        swap.wait_send()

    wait_for(rs_in.at[pl.ds(0, slices - 1)], rs_send)

    def arrived(d, carry):
        there = (tm + d) % slices
        wait_for(ag.at[there], ag_recv.at[there])
        return carry

    lax.fori_loop(1, slices, arrived, 0)
    for t in range(tiles):
        rows, lanes = slice(t // wide * 8, t // wide * 8 + 8), slice(t % wide * 128, t % wide * 128 + 128)
        out[rows, lanes] = ag[t // per, t % per]

    wait_for(ag.at[pl.ds(0, slices - 1)], ag_send)


def per_device(side, xs, slices, states, vectors, kernel_scale, neighbour_blocks, neighbour_count):
    coords, own = states.shape[1:]
    vecs = vectors.shape[0]
    chips = side * side
    tiles = vecs * own // 1024
    vmem = pl.BlockSpec(memory_space=pltpu.VMEM)
    hbm = pl.BlockSpec(memory_space=pltpu.HBM)
    dma = pltpu.SemaphoreType.DMA
    return pl.pallas_call(
        functools.partial(kernel, side, xs, slices),
        out_shape=pltpu.VMEM((vecs, own), jnp.float32),
        in_specs=[hbm] * 5,
        out_specs=vmem,
        scratch_shapes=[
            pltpu.VMEM((coords, own), jnp.float32),
            pltpu.SMEM((1,), jnp.float32),
            pltpu.VMEM(neighbour_blocks.shape, jnp.int32),
            pltpu.SMEM(neighbour_count.shape, jnp.int32),
            pltpu.VMEM((chips, coords, own), jnp.int16),
            pltpu.VMEM((coords, own), jnp.int16),
            pltpu.VMEM((chips, 1, 128), jnp.int32),
            pltpu.VMEM((1, 128), jnp.int32),
            pltpu.VMEM((chips, vecs, own), jnp.bfloat16),
            pltpu.VMEM((chips, vecs, own), jnp.bfloat16),
            pltpu.VMEM((4 * coords + 16, 2 * own), jnp.bfloat16),
            pltpu.VMEM((chips, 8, 2 * own), jnp.float32),
            pltpu.VMEM((chips, 8, 2 * own), jnp.float32),
            pltpu.VMEM((chips, own, 2 * own), jnp.bfloat16),
            pltpu.VMEM((chips, own, 2 * own), jnp.bfloat16),
            pltpu.VMEM((8, 2 * own), jnp.float32),
            pltpu.VMEM((vecs, 2 * own), jnp.float32),
            pltpu.VMEM((2, vecs + 8, own), jnp.float32),
            pltpu.VMEM((2, vecs + 8, own), jnp.float32),
            pltpu.VMEM((tiles, 8, 128), jnp.float32),
            pltpu.VMEM((slices, tiles // slices, 8, 128), jnp.float32),
            pltpu.VMEM((slices, tiles // slices, 8, 128), jnp.float32),
            dma,
            dma((chips,)),
            dma,
            dma((chips,)),
            dma,
            dma((side,)),
            dma((side,)),
            dma((chips,)),
            dma,
            dma((chips,)),
            dma((4,)),
            dma((4,)),
            dma,
            dma((slices,)),
            dma,
            dma((slices,)),
            dma((5,)),
        ],
        compiler_params=pltpu.CompilerParams(
            collective_id=0, has_side_effects=True, vmem_limit_bytes=VMEM_KIB * 1024
        ),
    )(states, vectors, kernel_scale, neighbour_blocks, neighbour_count)


def solution(mesh):
    side, slices = math.isqrt(mesh.shape["traj"] // 2), mesh.shape["tm"]
    xs = min(side, slices)
    return jax.shard_map(
        functools.partial(per_device, side, xs, slices),
        mesh=mesh,
        in_specs=(P("tm", None, "traj"), P(None, "traj"), P("tm"), P("traj", None), P("traj")),
        out_specs=P(None, "traj"),
        check_vma=False,
    )
```
